1024 devices in a mesh: section: 4 (over x), dp: 16 (over z_lo), expert: 16 (over y, z_hi, core).
Axes of the slice: x: 4, y: 4, z: 32 (z_hi: 2, z_lo: 16; z = z_hi * 16 + z_lo), core: 2. Of those that a mesh axis runs over, the one named last changes fastest.
Arguments:
- tokens: bfloat16 [4, 6144, 1024], P('section', ('dp', 'expert')), may hold values from -24 to 24
- routes: int32 [4, 6144, 6], P('section', ('dp', 'expert')), may hold values from 0 to 31, all different within a row; in each aligned block of 24 rows (0 to 23, 24 to 47, ..., all dimensions but the last counted through in order) at most 6 rows name the same one
- gate_values: float32 [4, 6144, 6], P('section', ('dp', 'expert')), may hold values from 0.1 to 1
- up_weight: bfloat16 [4, 32, 1024, 704], P('section', 'expert'), may hold values from -0.1875 to 0.1875
- down_weight: bfloat16 [4, 32, 704, 1024], P('section', 'expert'), may hold values from -0.21875 to 0.21875
- out_grad: bfloat16 [4, 6144, 1024], P('section', ('dp', 'expert')), may hold values from -6 to 6
Outputs:
- layer_output: bfloat16 [4, 6144, 1024], P('section', ('dp', 'expert'))
- sent_grad: bfloat16 [4, 6144, 1024], P('section', ('dp', 'expert'))
- gate_grad: float32 [4, 6144, 6], P('section', ('dp', 'expert'))
- up_grad: bfloat16 [4, 32, 1024, 704], P('section', 'expert', 'dp')
- down_grad: bfloat16 [4, 32, 1024, 704], P('section', 'expert', 'dp')
The draws below stay inside these ranges and needn't reach their ends.
Inputs may be any that keep to these rules, and one draw needn't show every extreme that they name: `routes`: each token names 6 different experts. Within one layer, the 24 tokens of one device name no expert more than 6 times, and some device names some expert exactly 6 times.
All inputs are finite; a program needn't handle non-finite values.
Results may differ from the reference program's by a relative error of at most 0.022.
Values may be sent and summed in bfloat16 or wider, within the bound.
No kernel may reach another device: no remote copies, remote signals or barrier semaphores. Data moves between devices by JAX's collectives and lax.ppermute only.
A program may use at most 64 MiB of HBM per device.

```python
import math
import jax
import jax.numpy as jnp
import numpy as np
from jax import lax

D = 1024
HE = 704
TOP = 6
TOK_DEV = 24
LAYERS = 4
EXPERTS = 32
TOKENS = 6144
CAP = 6
N_DP = 16
N_EXPERT = 16


def spiked(entries, rng, source, target, blocks, factor):
    owner, partner = [(jnp.arange(entries.shape[dim]) // (entries.shape[dim] // blocks)).reshape([-1 if axis == dim else 1 for axis in range(entries.ndim)]) for dim in (source, target)]
    chosen = jax.random.permutation(rng, blocks)[partner]
    strong = (owner == chosen) | (owner == (partner + blocks // 2) % blocks)
    return jnp.where(strong, factor * entries, entries)


def steps_of(rng, extent, cuts, smallest, high):
    def one(dim, blocks):
        steps = jax.random.uniform(jax.random.fold_in(jax.random.fold_in(rng, 6), dim), (blocks,), jnp.float32, smallest / len(cuts), high / len(cuts))
        return jnp.repeat(jnp.exp(steps), extent[dim] // blocks).reshape((-1,) + (1,) * (len(extent) - dim - 1))

    level = one(*cuts[0])
    for cut in cuts[1:]:
        level = level * one(*cut)
    return level


def shared_out(stream_key, own, number, rows, amount, top, most, lean):
    ranking = jax.random.permutation(stream_key, amount)
    heavy_load, usual = load_shares(amount, rows * top, most, lean, True), load_shares(amount, rows * top, most, lean, False)
    places = jnp.arange(amount)

    def named(tallies, offset_by):
        used = int((tallies > 0).sum())
        fixed = max(1, used // 4)
        shifted = fixed + (places - fixed + offset_by * (used - fixed)) % max(1, amount - fixed)
        return jnp.zeros((amount,), jnp.int32).at[ranking[jnp.where(places < fixed, places, shifted)]].set(jnp.asarray(tallies, jnp.int32))

    tallies = jnp.where(number % 4 == 0, named(heavy_load, number // 4), named(usual, number - number // 4 - 1))
    mixed = jax.random.permutation(jax.random.fold_in(own, 3), amount)
    giver, taker = mixed[0:amount // 2 * 2:2], mixed[1:amount // 2 * 2:2]
    room = jnp.minimum(tallies[giver] - 1, most - tallies[taker]) // 2
    room = jnp.where((giver == ranking[0]) | (taker == ranking[0]) | (tallies[taker] == 0), 0, jnp.maximum(room, 0))
    shifted = jax.random.randint(jax.random.fold_in(own, 4), (amount // 2,), 0, 1 << 20) % (room + 1)
    tallies = tallies.at[giver].add(-shifted).at[taker].add(shifted)
    members = jnp.searchsorted(jnp.cumsum(tallies), jnp.arange(rows * top), side="right").astype(jnp.int32)
    table = members.reshape(top, rows).T
    table = table[jax.random.permutation(jax.random.fold_in(own, 1), rows)]
    offset_by = jax.random.randint(jax.random.fold_in(own, 2), (rows, 1), 0, top)
    return jnp.take_along_axis(table, (jnp.arange(top)[None, :] + offset_by) % top, axis=1)


def load_shares(amount, total, reach, skew, full):
    portions = [(1 << 20) // math.isqrt(standing ** skew) + 1 for standing in range(1, amount + 1)]
    largest = reach if full else min(reach, max(-(-total // amount), total * portions[0] // sum(portions)))
    least = 1 if total - largest >= amount - 1 else 0
    given, surplus = [largest] + [least] * (amount - 1), total - largest - least * (amount - 1)
    while surplus > 0:
        movable = [i for i in range(1, amount) if given[i] < largest] or [i for i in range(1, amount) if given[i] < reach]
        pool, budget = sum([portions[i] for i in movable]), surplus
        for i in movable:
            addition = min(reach - given[i], max(1, budget * portions[i] // pool), surplus)
            given[i] = given[i] + addition
            surplus = surplus - addition
    return np.array(given)


def noise(own_key, extent, deviation, bound, cuts=(), kind=jnp.bfloat16):
    array = deviation * jax.random.normal(own_key, extent, jnp.float32)
    if cuts:
        array = array * steps_of(own_key, extent, cuts, -0.22, 0.18)
    return jnp.clip(array, -bound, bound).astype(kind)


def bell_draw_with(own_key, dims, width, bound, shards, heavy, kind=jnp.bfloat16):
    array = width * jax.random.normal(own_key, dims, jnp.float32)
    if shards:
        array = array * steps_of(own_key, dims, shards, -0.22, 0.18)
    return jnp.clip(spiked(array, jax.random.fold_in(own_key, 3), *heavy), -bound, bound).astype(kind)


def setup_inputs(seed: int = 0) -> dict:
    key_list = jax.random.split(jax.random.key(seed), 7)
    tokens = bell_draw_with(key_list[0], (LAYERS, TOKENS, D), 1.0, 24.0, ((0, 4), (1, 256)), (1, 2, 256, 6.0))
    routes_keys = jax.random.split(jax.random.fold_in(key_list[1], 1), LAYERS * TOKENS // TOK_DEV)
    routes_turns = jax.random.permutation(jax.random.fold_in(key_list[1], 3), LAYERS * TOKENS // TOK_DEV)
    routes = jax.vmap(lambda own, number: shared_out(jax.random.fold_in(key_list[1], 2), own, number, TOK_DEV, EXPERTS, TOP, CAP, 2))(routes_keys, routes_turns).reshape((LAYERS, TOKENS, TOP))
    gate_values = jnp.clip(0.1 + 0.9 * jax.random.uniform(key_list[2], (LAYERS, TOKENS, TOP), jnp.float32) ** steps_of(key_list[2], (LAYERS, TOKENS, TOP), ((0, 4), (1, 256)), -0.2, 0.2), 0.1, 1.0)
    up_weight = noise(key_list[3], (LAYERS, EXPERTS, D, HE), D ** -0.5, 0.1875, ((0, 4), (1, 16)))
    down_weight = noise(key_list[4], (LAYERS, EXPERTS, HE, D), HE ** -0.5, 0.21875, ((0, 4), (1, 16)))
    out_grad = noise(key_list[5], (LAYERS, TOKENS, D), 1.0, 6.0, ((0, 4), (1, 256)))
    return {"tokens": tokens, "routes": routes, "gate_values": gate_values, "up_weight": up_weight, "down_weight": down_weight, "out_grad": out_grad}


def silu_slope(hidden):
    logistic = jax.nn.sigmoid(hidden)
    return logistic * (1.0 + hidden * (1.0 - logistic))


def slot_within(route_rows):
    matches = (route_rows[:, :, None] == jnp.arange(EXPERTS, dtype=jnp.int32)[None, None, :]).astype(jnp.int32)
    counts = jnp.cumsum(matches, axis=1).astype(jnp.int32)
    return (jnp.sum(matches * counts, axis=2).astype(jnp.int32) - 1).astype(jnp.int32)


def one_layer(tokens, routes, gate_values, up_weight, down_weight, out_grad):
    blocks = N_DP * N_EXPERT
    route_rows = routes.reshape(blocks, TOK_DEV * TOP).astype(jnp.int32)
    within = slot_within(route_rows)
    block_ids = jnp.arange(blocks, dtype=jnp.int32)[:, None]
    group_index = block_ids // N_EXPERT
    source = block_ids % N_EXPERT
    flat_index = ((((group_index * EXPERTS + route_rows) * N_EXPERT + source) * CAP + within).reshape(-1)).astype(jnp.int32)
    slot_total = N_DP * EXPERTS * N_EXPERT * CAP
    slot_shape = (N_DP, EXPERTS, N_EXPERT * CAP, D)
    token_route = jnp.repeat(tokens, TOP, axis=0)
    sent_inputs = jnp.zeros((slot_total, D), jnp.bfloat16).at[flat_index].set(token_route).reshape(slot_shape)
    up_float = up_weight.astype(jnp.float32)
    down_float = down_weight.astype(jnp.float32)
    hidden = jnp.einsum("gesd,edh->gesh", sent_inputs.astype(jnp.float32), up_float)
    activated = jax.nn.silu(hidden).astype(jnp.bfloat16)
    produced = jnp.einsum("gesh,ehd->gesd", activated.astype(jnp.float32), down_float).astype(jnp.bfloat16)
    picked = produced.reshape(slot_total, D)[flat_index].astype(jnp.float32).reshape(TOKENS, TOP, D)
    layer_output = jnp.sum(gate_values[:, :, None] * picked, axis=1).astype(jnp.bfloat16)
    grad_float = out_grad.astype(jnp.float32)
    gate_grad = jnp.sum(grad_float[:, None, :] * picked, axis=2)
    scaled = (gate_values[:, :, None] * grad_float[:, None, :]).astype(jnp.bfloat16).reshape(TOKENS * TOP, D)
    sent_grads = jnp.zeros((slot_total, D), jnp.bfloat16).at[flat_index].set(scaled).reshape(slot_shape)
    act_grad = jnp.einsum("gesd,ehd->gesh", sent_grads.astype(jnp.float32), down_float)
    hidden_grad = (act_grad * silu_slope(hidden)).astype(jnp.bfloat16)
    route_grad = jnp.einsum("gesh,edh->gesd", hidden_grad.astype(jnp.float32), up_float).astype(jnp.bfloat16)
    grads_back = route_grad.reshape(slot_total, D)[flat_index].astype(jnp.float32).reshape(TOKENS, TOP, D)
    input_grad = jnp.sum(grads_back, axis=1).astype(jnp.bfloat16)

    def add_group(running, pieces):
        group_inputs, group_hidden_grad, group_grads, group_activated = pieces
        up_part = jnp.einsum("esd,esh->edh", group_inputs.astype(jnp.float32), group_hidden_grad.astype(jnp.float32))
        down_part = jnp.einsum("esd,esh->edh", group_grads.astype(jnp.float32), group_activated.astype(jnp.float32))
        up_part = lax.optimization_barrier(up_part.astype(jnp.bfloat16)).astype(jnp.float32)
        down_part = lax.optimization_barrier(down_part.astype(jnp.bfloat16)).astype(jnp.float32)
        return (running[0] + up_part, running[1] + down_part), None

    start_sums = (jnp.zeros((EXPERTS, D, HE), jnp.float32), jnp.zeros((EXPERTS, D, HE), jnp.float32))
    totals, unused = lax.scan(add_group, start_sums, (sent_inputs, hidden_grad, sent_grads, activated))
    return layer_output, input_grad, gate_grad, totals[0].astype(jnp.bfloat16), totals[1].astype(jnp.bfloat16)


def reference(tokens, routes, gate_values, up_weight, down_weight, out_grad):
    collected = []
    for layer_index in range(LAYERS):
        collected.append(one_layer(tokens[layer_index], routes[layer_index], gate_values[layer_index],
                                   up_weight[layer_index], down_weight[layer_index], out_grad[layer_index]))
    layer_output = jnp.stack([item[0] for item in collected])
    input_grad = jnp.stack([item[1] for item in collected])
    gate_grad = jnp.stack([item[2] for item in collected])
    up_grad = jnp.stack([item[3] for item in collected])
    down_grad = jnp.stack([item[4] for item in collected])
    sent_grad = jnp.roll(input_grad, -1, axis=0)
    return (layer_output, sent_grad, gate_grad, up_grad, down_grad)
```

```python
import functools

import jax
import jax.numpy as jnp
from jax import lax
from jax.experimental import pallas as pl
from jax.experimental.pallas import tpu as pltpu
from jax.sharding import PartitionSpec as P

PLANE = ("dp", "expert")
ROUND = ("section", "dp", "expert")
LANES = 128
CAPACITY = 6
F32 = jnp.float32
BF16 = jnp.bfloat16

Z_LO, Y, Z_HI, CORES = 16, 4, 2, 2
Z = Z_LO * Z_HI
CLASS = 4


def place(z, y, core):
    return (z % Z_LO) * (Y * Z_HI * CORES) + y * (Z_HI * CORES) + (z // Z_LO) * CORES + core


def moved(dz=0, dy=0, flip=0):
    return [
        (place(z, y, c), place((z + dz) % Z, (y + dy) % Y, c ^ flip))
        for z in range(Z)
        for y in range(Y)
        for c in range(CORES)
    ]


def send(block, dz=0, dy=0, flip=0):
    return lax.ppermute(block, PLANE, moved(dz, dy, flip))


def send_in_block(block, flip):
    pairs = [
        (place(z, y, c), place(z ^ flip, y, c))
        for z in range(Z)
        for y in range(Y)
        for c in range(CORES)
    ]
    return lax.ppermute(block, PLANE, pairs)


def send_to_section_before(block, sections, dz=0):
    plane = Z * Y * CORES
    pairs = [
        (s * plane + a, ((s - 1) % sections) * plane + b)
        for s in range(sections)
        for a, b in moved(dz)
    ]
    return lax.ppermute(block, ROUND, pairs)


def dot(a, b, over):
    return lax.dot_general(a, b, (over, ((), ())), preferred_element_type=F32)


NN = ((1,), (0,))
NT = ((1,), (1,))
TN = ((0,), (0,))


def experts_kernel(
    place_ref, *refs, pieces, groups, tok, feat, units, features_out, capacity
):
    piece_refs = refs[:pieces]
    up_ref, down_ref, keep_ref, send_ref, parts_out, xs, gs, us, acts, hgs, sums = refs[pieces:]
    first = place_ref[0]
    column = place_ref[1]
    spot = place_ref[2]
    per_piece = 2 * tok
    rows = pieces * per_piece
    slots = rows // tok * capacity
    wide = 2 * LANES
    lane = lax.broadcasted_iota(jnp.int32, (rows, LANES), 1)
    r_row = lax.broadcasted_iota(jnp.int32, (rows, rows), 0)
    r_col = lax.broadcasted_iota(jnp.int32, (rows, rows), 1)
    before = jnp.where((r_col <= r_row) & (r_col // tok == r_row // tok), 1.0, 0.0).astype(BF16)
    ones = jnp.ones((LANES, wide), BF16)
    base = (lax.broadcasted_iota(jnp.int32, (rows, wide), 0) // tok * capacity - 1).astype(F32)
    lane_wide = lax.broadcasted_iota(jnp.int32, (rows, wide), 1).astype(F32)
    s_lane = lax.broadcasted_iota(jnp.int32, (slots, LANES), 1)
    names = [(first + j).astype(F32) for j in range(2)]
    own = None
    own_meta = []
    for g in range(groups):
        block = jnp.concatenate(
            [r[g * per_piece : (g + 1) * per_piece, :] for r in piece_refs], axis=0
        )
        meta = block[:, 2 * feat :].astype(F32)
        at = []
        for j in range(2):
            hit = jnp.where((meta == names[j]) & (lane < 6), 1.0, 0.0).astype(BF16)
            named = dot(hit, ones, NN)
            rank = dot(before, named.astype(BF16), NN)
            target = jnp.where(named > 0.5, base + rank + j * slots, -1.0)
            at.append(target)
        picks = jnp.where((at[0] == lane_wide) & (lane_wide < slots), 1.0, 0.0) + jnp.where(
            at[1] == lane_wide, 1.0, 0.0
        )
        picks = picks.astype(BF16)
        gathered = dot(picks, block, TN)
        for j in range(2):
            part = gathered[j * slots : (j + 1) * slots]
            m = part[:, 2 * feat :]
            gates = pltpu.roll(m, LANES - 16, 1)
            match = (m == names[j]) & (s_lane < 12)
            gate = jnp.sum(jnp.where(match, gates, 0.0), axis=1, keepdims=True)
            grad = part[:, feat : 2 * feat]
            xs[j, g * slots : (g + 1) * slots, :] = part[:, :feat].astype(BF16)
            gs[j, g * slots : (g + 1) * slots, :] = (gate * grad).astype(BF16)
            if g == 0:
                us[j] = grad
                own_meta.append((match, gate))
        if g == 0:
            own = picks
    back = []
    for j in range(2):
        hidden = dot(xs[j], up_ref[j], NT)
        logistic = 1.0 / (1.0 + jnp.exp(-hidden))
        act = (hidden * logistic).astype(BF16)
        slope = logistic * (1.0 + hidden * (1.0 - logistic))
        hg = (dot(gs[j], down_ref[j], NT) * slope).astype(BF16)
        acts[...] = act
        hgs[...] = hg
        match, gate = own_meta[j]
        out = dot(acts[:slots], down_ref[j], NN).astype(BF16).astype(F32)
        dots = jnp.sum(us[j] * out, axis=1, keepdims=True)
        high = dots.astype(BF16).astype(F32)
        d = jnp.where(match, jnp.where(s_lane < 6, high, dots - high), 0.0).astype(BF16)
        rg = dot(hgs[:slots], up_ref[j], NN).astype(BF16)
        back.append(jnp.concatenate([(gate * out).astype(BF16), rg, d], axis=1))
        cols = pl.ds(pl.multiple_of(column, 256), 256)
        up_part = dot(xs[j, :, cols], hgs[...], TN).astype(BF16)
        down_part = dot(gs[j, :, cols], acts[...], TN).astype(BF16)
        sums[0] = up_part
        sums[1] = down_part
        for q in range(CLASS):
            take = pl.ds(pl.multiple_of((spot ^ q) * features_out, features_out), features_out)
            parts_out[q, 0, j] = sums[0, take, :]
            parts_out[q, 1, j] = sums[1, take, :]
    pad = jnp.zeros((wide - 2 * slots, back[0].shape[1]), BF16)
    stacked = jnp.concatenate(back + [pad], axis=0)
    result = dot(own, stacked, NN).astype(BF16)
    keep_ref[...] = result[: rows // 2]
    send_ref[...] = result[rows // 2 :]


def run_experts(pieces, up_t, down, where, tok, feat, features_out):
    units = up_t.shape[1]
    width = pieces[0].shape[1]
    groups = pieces[0].shape[0] // (2 * tok)
    rows = len(pieces) * 2 * tok
    slots = rows // tok * CAPACITY
    kernel = functools.partial(
        experts_kernel,
        pieces=len(pieces),
        groups=groups,
        tok=tok,
        feat=feat,
        units=units,
        features_out=features_out,
        capacity=CAPACITY,
    )
    vmem = pl.BlockSpec(memory_space=pltpu.VMEM)
    return pl.pallas_call(
        kernel,
        out_shape=(
            jax.ShapeDtypeStruct((rows // 2, width), BF16),
            jax.ShapeDtypeStruct((rows // 2, width), BF16),
            jax.ShapeDtypeStruct((CLASS, 2, 2, features_out, units), BF16),
        ),
        in_specs=[pl.BlockSpec(memory_space=pltpu.SMEM)] + [vmem] * (len(pieces) + 2),
        out_specs=(vmem,) * 3,
        scratch_shapes=[
            pltpu.VMEM((2, groups * slots, feat), BF16),
            pltpu.VMEM((2, groups * slots, feat), BF16),
            pltpu.VMEM((2, slots, feat), F32),
            pltpu.VMEM((groups * slots, units), BF16),
            pltpu.VMEM((groups * slots, units), BF16),
            pltpu.VMEM((2, CLASS * features_out, units), BF16),
        ],
        compiler_params=pltpu.CompilerParams(vmem_limit_bytes=56 * 1024 * 1024),
        cost_estimate=pl.CostEstimate(
            flops=8 * 10**9, bytes_accessed=16 * 10**6, transcendentals=10**6
        ),
    )(where, *pieces, up_t, down)


def body(sections, tokens, routes, gate_values, up_weight, down_weight, out_grad):
    tok, feat = tokens.shape[1:]
    top = routes.shape[2]
    gates = gate_values[0]
    names = routes[0].astype(BF16)
    high = lax.reduce_precision(gates, 8, 7)
    gap = jnp.zeros((tok, 16 - 2 * top), BF16)
    meta = jnp.concatenate(
        [names, names, gap, high.astype(BF16), (gates - high).astype(BF16)], axis=1
    )
    meta = jnp.pad(meta, ((0, 0), (0, LANES - meta.shape[1])))
    mine = jnp.concatenate([tokens[0], out_grad[0], meta], axis=1)

    across = send(mine, dz=Z_LO)
    ups, downs = [mine], [mine]
    for _ in range(3):
        ups.append(send(ups[-1], dz=CLASS))
        downs.append(send(downs[-1], dz=-CLASS))
    line = jnp.concatenate(
        [mine, across, ups[1], downs[3], ups[2], downs[2], ups[3], downs[1]], axis=0
    )
    pieces = [line] + [send(line, dy=d) for d in range(1, Y)]
    pieces = pieces + [send(p, flip=1) for p in pieces]

    z_lo = lax.axis_index("dp")
    local = up_weight.shape[1]
    features_out = feat // Z_LO
    where = jnp.stack(
        [lax.axis_index("expert") * local, z_lo // CLASS * (CLASS * features_out), z_lo % CLASS]
    ).astype(jnp.int32)
    keep, give, parts = run_experts(
        pieces, jnp.swapaxes(up_weight[0], 1, 2), down_weight[0], where, tok, feat, features_out
    )

    got = send(give, flip=1)
    both = (keep.astype(F32) + got.astype(F32)).astype(BF16).reshape(Y, 2 * tok, -1)
    total = both[0].astype(F32)
    for d in range(1, Y):
        total = total + send(both[d], dy=-d).astype(F32)
    total = total.astype(BF16)
    near, far = total[:tok], total[tok:]
    outer = jnp.concatenate([far[:, :feat], far[:, 2 * feat :]], axis=1)
    outer = send(outer, dz=Z_LO).astype(F32)
    layer_output = (near[:, :feat].astype(F32) + outer[:, :feat]).astype(BF16)
    dots = near[:, 2 * feat :].astype(F32) + outer[:, feat:]
    gate_grad = dots[:, :top] + dots[:, top : 2 * top]
    input_grad = send_to_section_before(near[:, feat : 2 * feat], sections).astype(
        F32
    ) + send_to_section_before(far[:, feat : 2 * feat], sections, dz=Z_LO).astype(F32)

    sums = parts[0].astype(F32)
    for flip in range(1, CLASS):
        sums = sums + send_in_block(parts[flip], flip).astype(F32)
    sums = sums.astype(BF16)
    return (
        layer_output[None],
        input_grad.astype(BF16)[None],
        gate_grad[None],
        sums[0][None],
        sums[1][None],
    )


def solution(mesh):
    placed = (
        P("section", ("dp", "expert"), None),
        P("section", ("dp", "expert"), None),
        P("section", ("dp", "expert"), None),
        P("section", "expert", None, None),
        P("section", "expert", None, None),
        P("section", ("dp", "expert"), None),
    )
    return jax.shard_map(
        functools.partial(body, mesh.shape["section"]),
        mesh=mesh,
        in_specs=placed,
        out_specs=(
            P("section", ("dp", "expert"), None),
            P("section", ("dp", "expert"), None),
            P("section", ("dp", "expert"), None),
            P("section", "expert", "dp", None),
            P("section", "expert", "dp", None),
        ),
        check_vma=False,
    )
```

```python
import functools

import jax
import jax.numpy as jnp
from jax import lax
from jax.experimental import pallas as pl
from jax.experimental.pallas import tpu as pltpu
from jax.sharding import PartitionSpec as P

PLANE = ("dp", "expert")
ROUND = ("section", "dp", "expert")
LANES = 128
CAPACITY = 6
F32 = jnp.float32
BF16 = jnp.bfloat16

Z_LO, Y, Z_HI, CORES = 16, 4, 2, 2
Z = Z_LO * Z_HI
CLASS = 4


def place(z, y, core):
    return (z % Z_LO) * (Y * Z_HI * CORES) + y * (Z_HI * CORES) + (z // Z_LO) * CORES + core


def moved(dz=0, dy=0, flip=0):
    return [
        (place(z, y, c), place((z + dz) % Z, (y + dy) % Y, c ^ flip))
        for z in range(Z)
        for y in range(Y)
        for c in range(CORES)
    ]


def send(block, dz=0, dy=0, flip=0):
    return lax.ppermute(block, PLANE, moved(dz, dy, flip))


LINES = [(y, c) for y in range(Y) for c in range(CORES)]
Z_CLASSES = [
    [place(z, y, c) for z in range(r, Z, CLASS)] for r in range(CLASS) for y, c in LINES
]
Z_BLOCKS = [
    [place(z + q, y, c) for q in range(CLASS)] for z in range(0, Z, CLASS) for y, c in LINES
]
Y_RINGS = [[place(z, y, c) for y in range(Y)] for z in range(Z) for c in range(CORES)]


def gather(block, rings):
    return lax.all_gather(block, PLANE, axis=0, tiled=True, axis_index_groups=rings)


def scatter_sum(block, rings):
    return lax.psum_scatter(
        block, PLANE, scatter_dimension=0, tiled=True, axis_index_groups=rings
    )


def send_to_section_before(block, sections, dz=0):
    plane = Z * Y * CORES
    pairs = [
        (s * plane + a, ((s - 1) % sections) * plane + b)
        for s in range(sections)
        for a, b in moved(dz)
    ]
    return lax.ppermute(block, ROUND, pairs)


def dot(a, b, over):
    return lax.dot_general(a, b, (over, ((), ())), preferred_element_type=F32)


NN = ((1,), (0,))
NT = ((1,), (1,))
TN = ((0,), (0,))


def experts_kernel(
    place_ref, near_ref, over_ref, up_hbm, down_hbm, keep_ref, send_ref, parts_out,
    up_ref, down_ref, xs, gs, us, picked, metas, acts, hgs, arrived, *, groups, tok, feat, capacity
):
    first = place_ref[0]
    block_at = place_ref[1]
    up_copy = pltpu.make_async_copy(up_hbm, up_ref, arrived.at[0])
    down_copy = pltpu.make_async_copy(down_hbm, down_ref, arrived.at[1])
    up_copy.start()
    down_copy.start()
    line = 2 * groups * tok
    rows = CORES * Y * 2 * tok
    slots = rows // tok * capacity
    wide = 2 * LANES
    lane = lax.broadcasted_iota(jnp.int32, (rows, LANES), 1)
    r_row = lax.broadcasted_iota(jnp.int32, (rows, rows), 0)
    r_col = lax.broadcasted_iota(jnp.int32, (rows, rows), 1)
    before = jnp.where((r_col <= r_row) & (r_col // tok == r_row // tok), 1.0, 0.0).astype(BF16)
    ones = jnp.ones((LANES, wide), BF16)
    base = (lax.broadcasted_iota(jnp.int32, (rows, wide), 0) // tok * capacity - 1).astype(F32)
    lane_wide = lax.broadcasted_iota(jnp.int32, (rows, wide), 1).astype(F32)
    s_lane = lax.broadcasted_iota(jnp.int32, (slots, LANES), 1)
    names = [(first + j).astype(F32) for j in range(2)]
    for g in range(groups):
        block = jnp.concatenate(
            [
                ref[start : start + tok, :]
                for ref in (near_ref, over_ref)
                for y in range(Y)
                for start in (y * line + g * tok, y * line + (g + groups) * tok)
            ],
            axis=0,
        )
        meta = block[:, 2 * feat :].astype(F32)
        at = []
        for j in range(2):
            hit = jnp.where((meta == names[j]) & (lane < 6), 1.0, 0.0).astype(BF16)
            named = dot(hit, ones, NN)
            rank = dot(before, named.astype(BF16), NN)
            at.append(jnp.where(named > 0.5, base + rank + j * slots, -1.0))
        picks = jnp.where((at[0] == lane_wide) & (lane_wide < slots), 1.0, 0.0) + jnp.where(
            at[1] == lane_wide, 1.0, 0.0
        )
        picks = picks.astype(BF16)
        picked[g] = picks
        gathered = dot(picks, block, TN)
        for j in range(2):
            here = slice(g * slots, (g + 1) * slots)
            part = gathered[j * slots : (j + 1) * slots]
            m = part[:, 2 * feat :]
            gates = pltpu.roll(m, LANES - 16, 1)
            match = (m == names[j]) & (s_lane < 12)
            gate = jnp.sum(jnp.where(match, gates, 0.0), axis=1, keepdims=True)
            grad = part[:, feat : 2 * feat]
            xs[j, here, :] = part[:, :feat].astype(BF16)
            us[j, here, :] = grad.astype(BF16)
            gs[j, here, :] = (gate * grad).astype(BF16)
            metas[j, here, :] = jnp.where(match, gate, 0.0)
    own = pl.ds(pl.multiple_of(block_at * slots, slots), slots)
    columns = feat // groups
    cols = pl.ds(pl.multiple_of(block_at * columns, columns), columns)
    each = columns // CLASS
    up_copy.wait()
    down_copy.wait()
    back = []
    for j in range(2):
        hidden = dot(xs[j], up_ref[j], NT)
        logistic = 1.0 / (1.0 + jnp.exp(-hidden))
        act = (hidden * logistic).astype(BF16)
        slope = logistic * (1.0 + hidden * (1.0 - logistic))
        hg = (dot(gs[j], down_ref[j], NT) * slope).astype(BF16)
        acts[...] = act
        hgs[...] = hg
        kept = metas[j, own, :]
        gate = jnp.max(kept, axis=1, keepdims=True)
        out = dot(acts[own, :], down_ref[j], NN).astype(BF16).astype(F32)
        dots = jnp.sum(us[j, own, :].astype(F32) * out, axis=1, keepdims=True)
        high = dots.astype(BF16).astype(F32)
        d = jnp.where(kept > 0.0, jnp.where(s_lane < 6, high, dots - high), 0.0).astype(BF16)
        rg = dot(hgs[own, :], up_ref[j], NN).astype(BF16)
        back.append(jnp.concatenate([(gate * out).astype(BF16), rg, d], axis=1))
        up_part = dot(xs[j, :, cols], hgs[...], TN).astype(BF16)
        down_part = dot(gs[j, :, cols], acts[...], TN).astype(BF16)
        for q in range(CLASS):
            parts_out[q, 0, j] = up_part[q * each : (q + 1) * each]
            parts_out[q, 1, j] = down_part[q * each : (q + 1) * each]
    pad = jnp.zeros((wide - 2 * slots, back[0].shape[1]), BF16)
    stacked = jnp.concatenate(back + [pad], axis=0)
    result = dot(picked[block_at], stacked, NN).astype(BF16)
    keep_ref[...] = result[: rows // 2]
    send_ref[...] = result[rows // 2 :]


def run_experts(near, over, up_t, down, where, tok, feat):
    units = up_t.shape[1]
    width = near.shape[1]
    groups = near.shape[0] // (Y * 2 * tok)
    rows = CORES * Y * 2 * tok
    slots = rows // tok * CAPACITY
    kernel = functools.partial(
        experts_kernel, groups=groups, tok=tok, feat=feat, capacity=CAPACITY
    )
    vmem = pl.BlockSpec(memory_space=pltpu.VMEM)
    anywhere = pl.BlockSpec(memory_space=pl.ANY)
    return pl.pallas_call(
        kernel,
        out_shape=(
            jax.ShapeDtypeStruct((rows // 2, width), BF16),
            jax.ShapeDtypeStruct((rows // 2, width), BF16),
            jax.ShapeDtypeStruct((CLASS, 2, 2, feat // Z_LO, units), BF16),
        ),
        in_specs=[pl.BlockSpec(memory_space=pltpu.SMEM), vmem, vmem, anywhere, anywhere],
        out_specs=(vmem,) * 3,
        scratch_shapes=[
            pltpu.VMEM((2, units, feat), BF16),
            pltpu.VMEM((2, units, feat), BF16),
            pltpu.VMEM((2, groups * slots, feat), BF16),
            pltpu.VMEM((2, groups * slots, feat), BF16),
            pltpu.VMEM((2, groups * slots, feat), BF16),
            pltpu.VMEM((groups, rows, 2 * LANES), BF16),
            pltpu.VMEM((2, groups * slots, LANES), F32),
            pltpu.VMEM((groups * slots, units), BF16),
            pltpu.VMEM((groups * slots, units), BF16),
            pltpu.SemaphoreType.DMA((2,)),
        ],
        compiler_params=pltpu.CompilerParams(vmem_limit_bytes=52 * 1024 * 1024),
        cost_estimate=pl.CostEstimate(
            flops=8 * 10**9, bytes_accessed=16 * 10**6, transcendentals=10**6
        ),
    )(where, near, over, up_t, down)


def body(sections, tokens, routes, gate_values, up_weight, down_weight, out_grad):
    tok, feat = tokens.shape[1:]
    top = routes.shape[2]
    gates = gate_values[0]
    names = routes[0].astype(BF16)
    high = lax.reduce_precision(gates, 8, 7)
    gap = jnp.zeros((tok, 16 - 2 * top), BF16)
    meta = jnp.concatenate(
        [names, names, gap, high.astype(BF16), (gates - high).astype(BF16)], axis=1
    )
    meta = jnp.pad(meta, ((0, 0), (0, LANES - meta.shape[1])))
    mine = jnp.concatenate([tokens[0], out_grad[0], meta], axis=1)

    line = gather(mine, Z_CLASSES)
    near = gather(line, Y_RINGS)
    over = send(near, flip=1)

    z_lo = lax.axis_index("dp")
    position = lax.axis_index("expert")
    where = jnp.stack([position * up_weight.shape[1], z_lo // CLASS]).astype(jnp.int32)
    keep, give, parts = run_experts(
        near, over, jnp.swapaxes(up_weight[0], 1, 2), down_weight[0], where, tok, feat
    )

    both = (keep.astype(F32) + send(give, flip=1).astype(F32)).astype(BF16)
    total = scatter_sum(both, Y_RINGS)
    lower = (position // CORES) % Z_HI == 0
    inner = jnp.where(lower, total[:tok], total[tok:])
    outer = jnp.where(lower, total[tok:], total[:tok])
    beyond = jnp.concatenate([outer[:, :feat], outer[:, 2 * feat :]], axis=1)
    beyond = send(beyond, dz=Z_LO).astype(F32)
    layer_output = (inner[:, :feat].astype(F32) + beyond[:, :feat]).astype(BF16)
    dots = inner[:, 2 * feat :].astype(F32) + beyond[:, feat:]
    gate_grad = dots[:, :top] + dots[:, top : 2 * top]
    input_grad = send_to_section_before(inner[:, feat : 2 * feat], sections).astype(
        F32
    ) + send_to_section_before(outer[:, feat : 2 * feat], sections, dz=Z_LO).astype(F32)

    shape = parts.shape
    parts = parts.reshape(-1, shape[-1])
    parts, total = lax.optimization_barrier((parts, total))
    sums = scatter_sum(parts, Z_BLOCKS).reshape(shape[1:])
    return (
        layer_output[None],
        input_grad.astype(BF16)[None],
        gate_grad[None],
        sums[0][None],
        sums[1][None],
    )


def solution(mesh):
    placed = (
        P("section", ("dp", "expert"), None),
        P("section", ("dp", "expert"), None),
        P("section", ("dp", "expert"), None),
        P("section", "expert", None, None),
        P("section", "expert", None, None),
        P("section", ("dp", "expert"), None),
    )
    return jax.shard_map(
        functools.partial(body, mesh.shape["section"]),
        mesh=mesh,
        in_specs=placed,
        out_specs=(
            P("section", ("dp", "expert"), None),
            P("section", ("dp", "expert"), None),
            P("section", ("dp", "expert"), None),
            P("section", "expert", "dp", None),
            P("section", "expert", "dp", None),
        ),
        check_vma=False,
    )
```

```python
import functools

import jax
import jax.numpy as jnp
from jax import lax
from jax.experimental import pallas as pl
from jax.experimental.pallas import tpu as pltpu
from jax.sharding import PartitionSpec as P

PLANE = ("dp", "expert")
ROUND = ("section", "dp", "expert")
LANES = 128
GATES_AT = 32
CAPACITY = 6
F32 = jnp.float32
BF16 = jnp.bfloat16

Z_LO, Y, Z_HI, CORES = 16, 4, 2, 2
Z = Z_LO * Z_HI
CLASS = 4
GROUPS = Z_LO // CLASS


def place(z, y, core):
    return (z % Z_LO) * (Y * Z_HI * CORES) + y * (Z_HI * CORES) + (z // Z_LO) * CORES + core


def moved(dz=0, dy=0, flip=0, block_flip=0):
    return [
        (place(z, y, c), place(((z ^ block_flip) + dz) % Z, (y + dy) % Y, c ^ flip))
        for z in range(Z)
        for y in range(Y)
        for c in range(CORES)
    ]


def send(block, **route):
    return lax.ppermute(block, PLANE, moved(**route))


LINES = [(y, c) for y in range(Y) for c in range(CORES)]
Z_CLASSES = [
    [place(z, y, c) for z in range(r, Z, CLASS)] for r in range(CLASS) for y, c in LINES
]
Y_RINGS = [[place(z, y, c) for y in range(Y)] for z in range(Z) for c in range(CORES)]


def gather(block, rings):
    return lax.all_gather(block, PLANE, axis=0, tiled=True, axis_index_groups=rings)


def send_to_section_before(block, sections, **route):
    plane = Z * Y * CORES
    pairs = [
        (s * plane + a, ((s - 1) % sections) * plane + b)
        for s in range(sections)
        for a, b in moved(**route)
    ]
    return lax.ppermute(block, ROUND, pairs)


def dot(a, b, over):
    return lax.dot_general(a, b, (over, ((), ())), preferred_element_type=F32)


NN = ((1,), (0,))
NT = ((1,), (1,))
TN = ((0,), (0,))


def constants(rows, tok, slots, experts, top):
    lanes = experts * slots
    r_row = lax.broadcasted_iota(jnp.int32, (rows, rows), 0)
    r_col = lax.broadcasted_iota(jnp.int32, (rows, rows), 1)
    before = (r_col <= r_row) & (r_col // tok == r_row // tok)
    m_row = lax.broadcasted_iota(jnp.int32, (LANES, lanes), 0)
    m_col = lax.broadcasted_iota(jnp.int32, (LANES, lanes), 1)
    row = lax.broadcasted_iota(jnp.int32, (rows, lanes), 0)
    lane = lax.broadcasted_iota(jnp.int32, (rows, lanes), 1)
    return (
        jnp.where(before, 1.0, 0.0).astype(BF16),
        jnp.where(m_row // top == m_col // slots, 1.0, 0.0).astype(BF16),
        (lane % slots - row // tok * CAPACITY + 1).astype(F32),
    )


def slot_picks(meta, names, top, consts):
    before, spread, wanted = consts
    lane = lax.broadcasted_iota(jnp.int32, meta.shape, 1)
    name = jnp.full(meta.shape, -1.0, F32)
    for e, value in enumerate(names):
        name = jnp.where((lane >= e * top) & (lane < (e + 1) * top), value, name)
    hit = jnp.where(meta.astype(F32) == name, 1.0, 0.0).astype(BF16)
    named = dot(hit, spread, NN)
    rank = dot(before, named.astype(BF16), NN)
    return jnp.where((named > 0.5) & (rank == wanted), 1.0, 0.0).astype(BF16)


def slot_gate(m, name, top):
    lane = lax.broadcasted_iota(jnp.int32, m.shape, 1)
    gates = pltpu.roll(m, LANES - GATES_AT, 1)
    match = (m == name) & (lane < 2 * top)
    return match, jnp.sum(jnp.where(match, gates, 0.0), axis=1, keepdims=True)


def through_expert(x, grad, up, down):
    hidden = dot(x, up, NT)
    logistic = 1.0 / (1.0 + jnp.exp(-hidden))
    slope = logistic * (1.0 + hidden * (1.0 - logistic))
    act = (hidden * logistic).astype(BF16)
    return act, (dot(grad, down, NT) * slope).astype(BF16)


def experts_kernel(
    place_ref, line, left, right, far_left, far_right,
    up_own, down_own, up_other, down_other, back_out, keep_out, give_out,
    rows_ref, up_ref, down_ref, xs, gs, us, picked, metas, acts, hgs, result_ref, sums,
    landed, arrived, *, tok, feat, local, top,
):
    experts = CORES * local
    names = [place_ref[e].astype(F32) for e in range(experts)]
    block_at, y_at, spot = place_ref[experts], place_ref[experts + 1], place_ref[experts + 2]
    span = GROUPS * tok
    landings = [
        pltpu.make_async_copy(line, rows_ref.at[0], landed.at[0]),
        pltpu.make_async_copy(left, rows_ref.at[1], landed.at[1]),
        pltpu.make_async_copy(far_left, rows_ref.at[2, pl.ds(0, span)], landed.at[2]),
        pltpu.make_async_copy(far_right, rows_ref.at[2, pl.ds(span, span)], landed.at[3]),
        pltpu.make_async_copy(right, rows_ref.at[3], landed.at[4]),
    ]
    copies = []
    for a, (up, down) in enumerate(((up_own, down_own), (up_other, down_other))):
        here = pl.ds(a * local, local)
        copies.append(pltpu.make_async_copy(up, up_ref.at[here], arrived.at[0, a]))
        copies.append(pltpu.make_async_copy(down, down_ref.at[here], arrived.at[1, a]))
    for copy in landings + copies:
        copy.start()
    sources = [(d, h * span) for d in range(Y) for h in range(Z_HI)]
    rows = len(sources) * tok
    slots = len(sources) * CAPACITY
    consts = constants(rows, tok, slots, experts, top)
    for copy in landings:
        copy.wait()
    for g in range(GROUPS):
        block = jnp.concatenate(
            [rows_ref[d, start + g * tok : start + (g + 1) * tok, :] for d, start in sources],
            axis=0,
        )
        picks = slot_picks(block[:, 2 * feat :], names, top, consts)
        picked[g] = picks
        gathered = dot(picks, block, TN)
        for e in range(experts):
            here = slice(g * slots, (g + 1) * slots)
            part = gathered[e * slots : (e + 1) * slots]
            match, gate = slot_gate(part[:, 2 * feat :], names[e], top)
            grad = part[:, feat : 2 * feat]
            xs[e, here, :] = part[:, :feat].astype(BF16)
            us[e, here, :] = grad.astype(BF16)
            gs[e, here, :] = (gate * grad).astype(BF16)
            metas[e, here, :] = jnp.where(match, gate, 0.0)
    s_lane = lax.broadcasted_iota(jnp.int32, (slots, LANES), 1)
    own = pl.ds(pl.multiple_of(block_at * slots, slots), slots)
    columns = feat // GROUPS
    cols = pl.ds(pl.multiple_of(block_at * columns, columns), columns)
    each = columns // CLASS
    back = []
    for a in range(CORES):
        copies[2 * a].wait()
        copies[2 * a + 1].wait()
        for j in range(local):
            e = a * local + j
            act, hg = through_expert(xs[e], gs[e], up_ref[e], down_ref[e])
            acts[...] = act
            hgs[...] = hg
            kept = metas[e, own, :]
            gate = jnp.max(kept, axis=1, keepdims=True)
            out = dot(acts[own, :], down_ref[e], NN).astype(BF16).astype(F32)
            dots = jnp.sum(us[e, own, :].astype(F32) * out, axis=1, keepdims=True)
            high = dots.astype(BF16).astype(F32)
            d = jnp.where(kept > 0.0, jnp.where(s_lane < top, high, dots - high), 0.0)
            rg = dot(hgs[own, :], up_ref[e], NN).astype(BF16)
            back.append(jnp.concatenate([(gate * out).astype(BF16), d.astype(BF16), rg], axis=1))
            for m, (side, value) in enumerate(((xs, hgs), (gs, acts))):
                sums[...] = dot(side[e, :, cols], value[...], TN).astype(BF16)
                for q in range(CLASS):
                    take = pl.ds(pl.multiple_of((spot ^ q) * each, each), each)
                    (keep_out, give_out)[a][q % 2, q // 2, m, j] = sums[take, :]
    stacked = jnp.concatenate(back, axis=0)
    result_ref[...] = dot(picked[block_at], stacked, NN).astype(BF16)
    share = rows // Y
    for y in range(Y):
        start = pl.multiple_of(((y_at + Y - y) % Y) * share, share)
        back_out[y * share : (y + 1) * share, :] = result_ref[pl.ds(start, share), :]


VMEM = pl.BlockSpec(memory_space=pltpu.VMEM)
HBM = pl.BlockSpec(memory_space=pltpu.HBM)
SCALARS = pl.BlockSpec(memory_space=pltpu.SMEM)


def run_experts(pieces, weights, where, tok, feat, top):
    local, units, _ = weights[0].shape
    width = pieces[0].shape[1]
    experts = CORES * local
    rows = pieces[0].shape[0] // GROUPS * Y
    slots = rows // tok * CAPACITY
    parts = jax.ShapeDtypeStruct((2, 2, 2, local, feat // Z_LO, units), BF16)
    return pl.pallas_call(
        functools.partial(experts_kernel, tok=tok, feat=feat, local=local, top=top),
        out_shape=(
            jax.ShapeDtypeStruct((rows, width), BF16),
            parts,
            parts,
        ),
        in_specs=[SCALARS] + [HBM] * (len(pieces) + len(weights)),
        out_specs=(VMEM,) * 3,
        scratch_shapes=[
            pltpu.VMEM((Y, pieces[0].shape[0], width), BF16),
            pltpu.VMEM((experts, units, feat), BF16),
            pltpu.VMEM((experts, units, feat), BF16),
            pltpu.VMEM((experts, GROUPS * slots, feat), BF16),
            pltpu.VMEM((experts, GROUPS * slots, feat), BF16),
            pltpu.VMEM((experts, GROUPS * slots, feat), BF16),
            pltpu.VMEM((GROUPS, rows, experts * slots), BF16),
            pltpu.VMEM((experts, GROUPS * slots, LANES), F32),
            pltpu.VMEM((GROUPS * slots, units), BF16),
            pltpu.VMEM((GROUPS * slots, units), BF16),
            pltpu.VMEM((rows, width), BF16),
            pltpu.VMEM((feat // GROUPS, units), BF16),
            pltpu.SemaphoreType.DMA((len(pieces),)),
            pltpu.SemaphoreType.DMA((2, CORES)),
        ],
        compiler_params=pltpu.CompilerParams(vmem_limit_bytes=44 * 1024 * 1024),
        cost_estimate=pl.CostEstimate(
            flops=12 * 10**9, bytes_accessed=20 * 10**6, transcendentals=10**6
        ),
    )(where, *pieces, *weights)


def both_halves(kept, got):
    return (kept.astype(F32) + got.astype(F32)).astype(BF16)


def body(sections, tokens, routes, gate_values, up_weight, down_weight, out_grad):
    tok, feat = tokens.shape[1:]
    top = routes.shape[2]
    gates = gate_values[0]
    names = routes[0].astype(BF16)
    high = lax.reduce_precision(gates, 8, 7)
    copies = CORES * up_weight.shape[1]
    gap = jnp.zeros((tok, GATES_AT - copies * top), BF16)
    meta = jnp.concatenate(
        [names] * copies + [gap, high.astype(BF16), (gates - high).astype(BF16)], axis=1
    )
    meta = jnp.pad(meta, ((0, 0), (0, LANES - meta.shape[1])))
    mine = jnp.concatenate([tokens[0], out_grad[0], meta], axis=1)

    z_lo = lax.axis_index("dp")
    position = lax.axis_index("expert")
    local = up_weight.shape[1]
    other = position + 1 - 2 * (position % CORES)
    first = [p * local + j for p in (position, other) for j in range(local)]
    y_at = position // (CORES * Z_HI)
    where = jnp.stack(first + [z_lo // CLASS, y_at, z_lo % CLASS]).astype(jnp.int32)
    up_t, down = jnp.swapaxes(up_weight[0], 1, 2), down_weight[0]

    line = gather(mine, Z_CLASSES)
    middle = line.shape[0] // 2
    left, right = send(line, dy=1), send(line, dy=-1)
    far_left, far_right = send(left[:middle], dy=1), send(right[middle:], dy=-1)
    weights = [up_t, down]
    up_t, down, _ = lax.optimization_barrier((up_t, down, line))
    weights = weights + [send(up_t, flip=1), send(down, flip=1)]
    back, keep, give = run_experts(
        [line, left, right, far_left, far_right], weights, where, tok, feat, top
    )

    share = back.shape[0] // Y
    spread = lax.all_to_all(back, PLANE, 0, 0, tiled=True, axis_index_groups=Y_RINGS)
    total = jnp.sum(spread.reshape(Y, share, -1).astype(F32), axis=0).astype(BF16)
    below = (position // CORES) % Z_HI == 0
    inner = jnp.where(below, total[:tok], total[tok:])
    outer = jnp.where(below, total[tok:], total[:tok])

    got = send(give, flip=1)
    give = both_halves(keep[1], got[1])
    keep = both_halves(keep[0], got[0])
    got = send(give, block_flip=1)
    give = both_halves(keep[1], got[1])
    keep = both_halves(keep[0], got[0])
    last = send(give, block_flip=2)
    beyond = send(outer, dz=Z_LO)
    beyond, last = lax.optimization_barrier((beyond, last))
    added = inner.astype(F32) + beyond.astype(F32)
    dots = added[:, feat : feat + LANES]
    gate_grad = dots[:, :top] + dots[:, top : 2 * top]
    input_grad = send_to_section_before(added[:, feat + LANES :].astype(BF16), sections)
    sums = both_halves(keep, last)
    return (
        added[:, :feat].astype(BF16)[None],
        input_grad[None],
        gate_grad[None],
        sums[0][None],
        sums[1][None],
    )


def solution(mesh):
    placed = (
        P("section", ("dp", "expert"), None),
        P("section", ("dp", "expert"), None),
        P("section", ("dp", "expert"), None),
        P("section", "expert", None, None),
        P("section", "expert", None, None),
        P("section", ("dp", "expert"), None),
    )
    return jax.shard_map(
        functools.partial(body, mesh.shape["section"]),
        mesh=mesh,
        in_specs=placed,
        out_specs=(
            P("section", ("dp", "expert"), None),
            P("section", ("dp", "expert"), None),
            P("section", ("dp", "expert"), None),
            P("section", "expert", "dp", None),
            P("section", "expert", "dp", None),
        ),
        check_vma=False,
    )
```

```python
import functools

import jax
import jax.numpy as jnp
from jax import lax
from jax.experimental import pallas as pl
from jax.experimental.pallas import tpu as pltpu
from jax.sharding import PartitionSpec as P

PLANE = ("dp", "expert")
ROUND = ("section", "dp", "expert")
LANES = 128
GATES_AT = 32
CAPACITY = 6
F32 = jnp.float32
BF16 = jnp.bfloat16

Z_LO, Y, Z_HI, CORES = 16, 4, 2, 2
Z = Z_LO * Z_HI
CLASS = 4
GROUPS = Z_LO // CLASS


def place(z, y, core):
    return (z % Z_LO) * (Y * Z_HI * CORES) + y * (Z_HI * CORES) + (z // Z_LO) * CORES + core


def moved(dz=0, dy=0, flip=0, block_flip=0):
    return [
        (place(z, y, c), place(((z ^ block_flip) + dz) % Z, (y + dy) % Y, c ^ flip))
        for z in range(Z)
        for y in range(Y)
        for c in range(CORES)
    ]


def send(block, **route):
    return lax.ppermute(block, PLANE, moved(**route))


LINES = [(y, c) for y in range(Y) for c in range(CORES)]
Z_CLASSES = [
    [place(z, y, c) for z in range(r, Z, CLASS)] for r in range(CLASS) for y, c in LINES
]
Y_RINGS = [[place(z, y, c) for y in range(Y)] for z in range(Z) for c in range(CORES)]


def gather(block, rings):
    return lax.all_gather(block, PLANE, axis=0, tiled=True, axis_index_groups=rings)


def send_to_section_before(block, sections, **route):
    plane = Z * Y * CORES
    pairs = [
        (s * plane + a, ((s - 1) % sections) * plane + b)
        for s in range(sections)
        for a, b in moved(**route)
    ]
    return lax.ppermute(block, ROUND, pairs)


def dot(a, b, over):
    return lax.dot_general(a, b, (over, ((), ())), preferred_element_type=F32)


NN = ((1,), (0,))
NT = ((1,), (1,))
TN = ((0,), (0,))


def constants(rows, tok, slots, experts, top):
    lanes = experts * slots
    r_row = lax.broadcasted_iota(jnp.int32, (rows, rows), 0)
    r_col = lax.broadcasted_iota(jnp.int32, (rows, rows), 1)
    before = (r_col <= r_row) & (r_col // tok == r_row // tok)
    m_row = lax.broadcasted_iota(jnp.int32, (LANES, lanes), 0)
    m_col = lax.broadcasted_iota(jnp.int32, (LANES, lanes), 1)
    row = lax.broadcasted_iota(jnp.int32, (rows, lanes), 0)
    lane = lax.broadcasted_iota(jnp.int32, (rows, lanes), 1)
    return (
        jnp.where(before, 1.0, 0.0).astype(BF16),
        jnp.where(m_row // top == m_col // slots, 1.0, 0.0).astype(BF16),
        (lane % slots - row // tok * CAPACITY + 1).astype(F32),
    )


def slot_picks(meta, names, top, consts):
    before, spread, wanted = consts
    lane = lax.broadcasted_iota(jnp.int32, meta.shape, 1)
    name = jnp.full(meta.shape, -1.0, F32)
    for e, value in enumerate(names):
        name = jnp.where((lane >= e * top) & (lane < (e + 1) * top), value, name)
    hit = jnp.where(meta.astype(F32) == name, 1.0, 0.0).astype(BF16)
    named = dot(hit, spread, NN)
    rank = dot(before, named.astype(BF16), NN)
    return jnp.where((named > 0.5) & (rank == wanted), 1.0, 0.0).astype(BF16)


def slot_gate(m, name, top):
    lane = lax.broadcasted_iota(jnp.int32, m.shape, 1)
    gates = pltpu.roll(m, LANES - GATES_AT, 1)
    match = (m == name) & (lane < 2 * top)
    return match, jnp.sum(jnp.where(match, gates, 0.0), axis=1, keepdims=True)


def through_expert(x, grad, up, down):
    hidden = dot(x, up, NT)
    logistic = 1.0 / (1.0 + jnp.exp(-hidden))
    slope = logistic * (1.0 + hidden * (1.0 - logistic))
    act = (hidden * logistic).astype(BF16)
    return act, (dot(grad, down, NT) * slope).astype(BF16)


def experts_kernel(
    place_ref, line, early, left, right, far_left, far_right,
    up_own, down_own, up_other, down_other, back_out, keep_out, give_out,
    rows_ref, up_ref, down_ref, xs, gs, us, picked, metas, acts, hgs, result_ref, sums,
    landed, arrived, *, tok, feat, local, top,
):
    experts = CORES * local
    names = [place_ref[e].astype(F32) for e in range(experts)]
    block_at, y_at, spot = place_ref[experts], place_ref[experts + 1], place_ref[experts + 2]
    span = GROUPS * tok
    head = early.shape[0] // Y
    far = far_left.shape[0]
    landings = [
        (line, rows_ref.at[0]),
        (left, rows_ref.at[1, pl.ds(head, left.shape[0])]),
        (far_left, rows_ref.at[2, pl.ds(head, far)]),
        (far_right, rows_ref.at[2, pl.ds(head + far, far_right.shape[0])]),
        (right, rows_ref.at[3, pl.ds(head, right.shape[0])]),
    ]
    for d in range(1, Y):
        start = pl.multiple_of(((y_at + Y - d) % Y) * head, head)
        landings.append((early.at[pl.ds(start, head)], rows_ref.at[d, pl.ds(0, head)]))
    landings = [
        pltpu.make_async_copy(source, target, landed.at[i])
        for i, (source, target) in enumerate(landings)
    ]
    copies = []
    for a, (up, down) in enumerate(((up_own, down_own), (up_other, down_other))):
        here = pl.ds(a * local, local)
        copies.append(pltpu.make_async_copy(up, up_ref.at[here], arrived.at[0, a]))
        copies.append(pltpu.make_async_copy(down, down_ref.at[here], arrived.at[1, a]))
    for copy in landings + copies:
        copy.start()
    sources = [(d, h * span) for d in range(Y) for h in range(Z_HI)]
    rows = len(sources) * tok
    slots = len(sources) * CAPACITY
    consts = constants(rows, tok, slots, experts, top)
    for copy in landings:
        copy.wait()
    for g in range(GROUPS):
        block = jnp.concatenate(
            [rows_ref[d, start + g * tok : start + (g + 1) * tok, :] for d, start in sources],
            axis=0,
        )
        picks = slot_picks(block[:, 2 * feat :], names, top, consts)
        picked[g] = picks
        gathered = dot(picks, block, TN)
        for e in range(experts):
            here = slice(g * slots, (g + 1) * slots)
            part = gathered[e * slots : (e + 1) * slots]
            match, gate = slot_gate(part[:, 2 * feat :], names[e], top)
            grad = part[:, feat : 2 * feat]
            xs[e, here, :] = part[:, :feat].astype(BF16)
            us[e, here, :] = grad.astype(BF16)
            gs[e, here, :] = (gate * grad).astype(BF16)
            metas[e, here, :] = jnp.where(match, gate, 0.0)
    s_lane = lax.broadcasted_iota(jnp.int32, (slots, LANES), 1)
    own = pl.ds(pl.multiple_of(block_at * slots, slots), slots)
    columns = feat // GROUPS
    cols = pl.ds(pl.multiple_of(block_at * columns, columns), columns)
    each = columns // CLASS
    back = []
    for a in range(CORES):
        copies[2 * a].wait()
        copies[2 * a + 1].wait()
        for j in range(local):
            e = a * local + j
            act, hg = through_expert(xs[e], gs[e], up_ref[e], down_ref[e])
            acts[...] = act
            hgs[...] = hg
            kept = metas[e, own, :]
            gate = jnp.max(kept, axis=1, keepdims=True)
            out = dot(acts[own, :], down_ref[e], NN).astype(BF16).astype(F32)
            dots = jnp.sum(us[e, own, :].astype(F32) * out, axis=1, keepdims=True)
            high = dots.astype(BF16).astype(F32)
            d = jnp.where(kept > 0.0, jnp.where(s_lane < top, high, dots - high), 0.0)
            rg = dot(hgs[own, :], up_ref[e], NN).astype(BF16)
            back.append(jnp.concatenate([(gate * out).astype(BF16), d.astype(BF16), rg], axis=1))
            for m, (side, value) in enumerate(((xs, hgs), (gs, acts))):
                sums[...] = dot(side[e, :, cols], value[...], TN).astype(BF16)
                for q in range(CLASS):
                    take = pl.ds(pl.multiple_of((spot ^ q) * each, each), each)
                    (keep_out, give_out)[a][q % 2, q // 2, m, j] = sums[take, :]
    stacked = jnp.concatenate(back, axis=0)
    result_ref[...] = dot(picked[block_at], stacked, NN).astype(BF16)
    share = rows // Y
    for y in range(Y):
        start = pl.multiple_of(((y_at + Y - y) % Y) * share, share)
        back_out[y * share : (y + 1) * share, :] = result_ref[pl.ds(start, share), :]


VMEM = pl.BlockSpec(memory_space=pltpu.VMEM)
HBM = pl.BlockSpec(memory_space=pltpu.HBM)
SCALARS = pl.BlockSpec(memory_space=pltpu.SMEM)


def run_experts(pieces, weights, where, tok, feat, top):
    local, units, _ = weights[0].shape
    width = pieces[0].shape[1]
    experts = CORES * local
    rows = pieces[0].shape[0] // GROUPS * Y
    slots = rows // tok * CAPACITY
    parts = jax.ShapeDtypeStruct((2, 2, 2, local, feat // Z_LO, units), BF16)
    return pl.pallas_call(
        functools.partial(experts_kernel, tok=tok, feat=feat, local=local, top=top),
        out_shape=(
            jax.ShapeDtypeStruct((rows, width), BF16),
            parts,
            parts,
        ),
        in_specs=[SCALARS] + [HBM] * (len(pieces) + len(weights)),
        out_specs=(VMEM,) * 3,
        scratch_shapes=[
            pltpu.VMEM((Y, pieces[0].shape[0], width), BF16),
            pltpu.VMEM((experts, units, feat), BF16),
            pltpu.VMEM((experts, units, feat), BF16),
            pltpu.VMEM((experts, GROUPS * slots, feat), BF16),
            pltpu.VMEM((experts, GROUPS * slots, feat), BF16),
            pltpu.VMEM((experts, GROUPS * slots, feat), BF16),
            pltpu.VMEM((GROUPS, rows, experts * slots), BF16),
            pltpu.VMEM((experts, GROUPS * slots, LANES), F32),
            pltpu.VMEM((GROUPS * slots, units), BF16),
            pltpu.VMEM((GROUPS * slots, units), BF16),
            pltpu.VMEM((rows, width), BF16),
            pltpu.VMEM((feat // GROUPS, units), BF16),
            pltpu.SemaphoreType.DMA((len(pieces) + 2,)),
            pltpu.SemaphoreType.DMA((2, CORES)),
        ],
        compiler_params=pltpu.CompilerParams(vmem_limit_bytes=44 * 1024 * 1024),
        cost_estimate=pl.CostEstimate(
            flops=12 * 10**9, bytes_accessed=20 * 10**6, transcendentals=10**6
        ),
    )(where, *pieces, *weights)


def both_halves(kept, got):
    return (kept.astype(F32) + got.astype(F32)).astype(BF16)


def body(sections, tokens, routes, gate_values, up_weight, down_weight, out_grad):
    tok, feat = tokens.shape[1:]
    top = routes.shape[2]
    gates = gate_values[0]
    names = routes[0].astype(BF16)
    high = lax.reduce_precision(gates, 8, 7)
    copies = CORES * up_weight.shape[1]
    gap = jnp.zeros((tok, GATES_AT - copies * top), BF16)
    meta = jnp.concatenate(
        [names] * copies + [gap, high.astype(BF16), (gates - high).astype(BF16)], axis=1
    )
    meta = jnp.pad(meta, ((0, 0), (0, LANES - meta.shape[1])))
    mine = jnp.concatenate([tokens[0], out_grad[0], meta], axis=1)

    z_lo = lax.axis_index("dp")
    position = lax.axis_index("expert")
    local = up_weight.shape[1]
    other = position + 1 - 2 * (position % CORES)
    first = [p * local + j for p in (position, other) for j in range(local)]
    y_at = position // (CORES * Z_HI)
    where = jnp.stack(first + [z_lo // CLASS, y_at, z_lo % CLASS]).astype(jnp.int32)
    up_t, down = jnp.swapaxes(up_weight[0], 1, 2), down_weight[0]

    line = gather(mine, Z_CLASSES)
    head = 2 * tok
    early = gather(line[:head], Y_RINGS)
    left, right = send(line[head:], dy=1), send(line[head:], dy=-1)
    middle = (line.shape[0] - head) // 32 * 16 + 16
    far_left, far_right = send(left[:middle], dy=1), send(right[middle:], dy=-1)
    weights = [up_t, down]
    up_t, down, _ = lax.optimization_barrier((up_t, down, line))
    weights = weights + [send(up_t, flip=1), send(down, flip=1)]
    back, keep, give = run_experts(
        [line, early, left, right, far_left, far_right], weights, where, tok, feat, top
    )

    share = back.shape[0] // Y
    spread = lax.all_to_all(back, PLANE, 0, 0, tiled=True, axis_index_groups=Y_RINGS)
    total = jnp.sum(spread.reshape(Y, share, -1).astype(F32), axis=0).astype(BF16)
    below = (position // CORES) % Z_HI == 0
    inner = jnp.where(below, total[:tok], total[tok:])
    outer = jnp.where(below, total[tok:], total[:tok])

    got = send(give, flip=1)
    give = both_halves(keep[1], got[1])
    keep = both_halves(keep[0], got[0])
    got = send(give, block_flip=1)
    give = both_halves(keep[1], got[1])
    keep = both_halves(keep[0], got[0])
    last = send(give, block_flip=2)
    beyond = send(outer, dz=Z_LO)
    beyond, give = lax.optimization_barrier((beyond, give))
    added = inner.astype(F32) + beyond.astype(F32)
    dots = added[:, feat : feat + LANES]
    gate_grad = dots[:, :top] + dots[:, top : 2 * top]
    input_grad = send_to_section_before(added[:, feat + LANES :].astype(BF16), sections)
    sums = both_halves(keep, last)
    return (
        added[:, :feat].astype(BF16)[None],
        input_grad[None],
        gate_grad[None],
        sums[0][None],
        sums[1][None],
    )


def solution(mesh):
    placed = (
        P("section", ("dp", "expert"), None),
        P("section", ("dp", "expert"), None),
        P("section", ("dp", "expert"), None),
        P("section", "expert", None, None),
        P("section", "expert", None, None),
        P("section", ("dp", "expert"), None),
    )
    return jax.shard_map(
        functools.partial(body, mesh.shape["section"]),
        mesh=mesh,
        in_specs=placed,
        out_specs=(
            P("section", ("dp", "expert"), None),
            P("section", ("dp", "expert"), None),
            P("section", ("dp", "expert"), None),
            P("section", "expert", "dp", None),
            P("section", "expert", "dp", None),
        ),
        check_vma=False,
    )
```

```python
import functools

import jax
import jax.numpy as jnp
from jax import lax
from jax.experimental import pallas as pl
from jax.experimental.pallas import tpu as pltpu
from jax.sharding import PartitionSpec as P

PLANE = ("dp", "expert")
ROUND = ("section", "dp", "expert")
LANES = 128
GATES_AT = 32
CAPACITY = 6
F32 = jnp.float32
BF16 = jnp.bfloat16

Z_LO, Y, Z_HI, CORES = 16, 4, 2, 2
Z = Z_LO * Z_HI
CLASS = 4
GROUPS = Z_LO // CLASS


def place(z, y, core):
    return (z % Z_LO) * (Y * Z_HI * CORES) + y * (Z_HI * CORES) + (z // Z_LO) * CORES + core


def moved(dz=0, dy=0, flip=0, block_flip=0):
    return [
        (place(z, y, c), place(((z ^ block_flip) + dz) % Z, (y + dy) % Y, c ^ flip))
        for z in range(Z)
        for y in range(Y)
        for c in range(CORES)
    ]


def send(block, **route):
    return lax.ppermute(block, PLANE, moved(**route))


LINES = [(y, c) for y in range(Y) for c in range(CORES)]
Z_CLASSES = [
    [place(z, y, c) for z in range(r, Z, CLASS)] for r in range(CLASS) for y, c in LINES
]
Y_RINGS = [[place(z, y, c) for y in range(Y)] for z in range(Z) for c in range(CORES)]


def gather(block, rings):
    return lax.all_gather(block, PLANE, axis=0, tiled=True, axis_index_groups=rings)


def send_to_section_before(block, sections, **route):
    plane = Z * Y * CORES
    pairs = [
        (s * plane + a, ((s - 1) % sections) * plane + b)
        for s in range(sections)
        for a, b in moved(**route)
    ]
    return lax.ppermute(block, ROUND, pairs)


def dot(a, b, over):
    return lax.dot_general(a, b, (over, ((), ())), preferred_element_type=F32)


NN = ((1,), (0,))
NT = ((1,), (1,))
TN = ((0,), (0,))


def constants(rows, tok, slots, experts, top):
    lanes = experts * slots
    r_row = lax.broadcasted_iota(jnp.int32, (rows, rows), 0)
    r_col = lax.broadcasted_iota(jnp.int32, (rows, rows), 1)
    before = (r_col <= r_row) & (r_col // tok == r_row // tok)
    m_row = lax.broadcasted_iota(jnp.int32, (LANES, lanes), 0)
    m_col = lax.broadcasted_iota(jnp.int32, (LANES, lanes), 1)
    row = lax.broadcasted_iota(jnp.int32, (rows, lanes), 0)
    lane = lax.broadcasted_iota(jnp.int32, (rows, lanes), 1)
    return (
        jnp.where(before, 1.0, 0.0).astype(BF16),
        jnp.where(m_row // top == m_col // slots, 1.0, 0.0).astype(BF16),
        (lane % slots - row // tok * CAPACITY + 1).astype(F32),
    )


def slot_picks(meta, names, top, consts):
    before, spread, wanted = consts
    lane = lax.broadcasted_iota(jnp.int32, meta.shape, 1)
    name = jnp.full(meta.shape, -1.0, F32)
    for e, value in enumerate(names):
        name = jnp.where((lane >= e * top) & (lane < (e + 1) * top), value, name)
    hit = jnp.where(meta.astype(F32) == name, 1.0, 0.0).astype(BF16)
    named = dot(hit, spread, NN)
    rank = dot(before, named.astype(BF16), NN)
    return jnp.where((named > 0.5) & (rank == wanted), 1.0, 0.0).astype(BF16)


def slot_gate(m, name, top):
    lane = lax.broadcasted_iota(jnp.int32, m.shape, 1)
    gates = pltpu.roll(m, LANES - GATES_AT, 1)
    match = (m == name) & (lane < 2 * top)
    return match, jnp.sum(jnp.where(match, gates, 0.0), axis=1, keepdims=True)


def through_expert(x, grad, up, down):
    hidden = dot(x, up, NT)
    logistic = 1.0 / (1.0 + jnp.exp(-hidden))
    slope = logistic * (1.0 + hidden * (1.0 - logistic))
    act = (hidden * logistic).astype(BF16)
    return act, (dot(grad, down, NT) * slope).astype(BF16)


def experts_kernel(
    place_ref, line, early, left, right, far_left, far_right,
    up_own, down_own, up_other, down_other, back_out, keep_out, give_out,
    rows_ref, up_ref, down_ref, xs, gs, us, picked, metas, acts, hgs, result_ref, sums,
    landed, arrived, *, tok, feat, local, top,
):
    experts = CORES * local
    names = [place_ref[e].astype(F32) for e in range(experts)]
    block_at, y_at, spot = place_ref[experts], place_ref[experts + 1], place_ref[experts + 2]
    span = GROUPS * tok
    head = early.shape[0] // Y
    far = far_left.shape[0]
    landings = [
        (line, rows_ref.at[0]),
        (left, rows_ref.at[1, pl.ds(head, left.shape[0])]),
        (far_left, rows_ref.at[2, pl.ds(head, far)]),
        (far_right, rows_ref.at[2, pl.ds(head + far, far_right.shape[0])]),
        (right, rows_ref.at[3, pl.ds(head, right.shape[0])]),
    ]
    for d in range(1, Y):
        start = pl.multiple_of(((y_at + Y - d) % Y) * head, head)
        landings.append((early.at[pl.ds(start, head)], rows_ref.at[d, pl.ds(0, head)]))
    landings = [
        pltpu.make_async_copy(source, target, landed.at[i])
        for i, (source, target) in enumerate(landings)
    ]
    copies = []
    for a, (up, down) in enumerate(((up_own, down_own), (up_other, down_other))):
        here = pl.ds(a * local, local)
        copies.append(pltpu.make_async_copy(up, up_ref.at[here], arrived.at[0, a]))
        copies.append(pltpu.make_async_copy(down, down_ref.at[here], arrived.at[1, a]))
    for copy in landings + copies:
        copy.start()
    sources = [(d, h * span) for d in range(Y) for h in range(Z_HI)]
    rows = len(sources) * tok
    slots = len(sources) * CAPACITY
    consts = constants(rows, tok, slots, experts, top)
    for copy in landings:
        copy.wait()
    for g in range(GROUPS):
        block = jnp.concatenate(
            [rows_ref[d, start + g * tok : start + (g + 1) * tok, :] for d, start in sources],
            axis=0,
        )
        picks = slot_picks(block[:, 2 * feat :], names, top, consts)
        picked[g] = picks
        gathered = dot(picks, block, TN)
        for e in range(experts):
            here = slice(g * slots, (g + 1) * slots)
            part = gathered[e * slots : (e + 1) * slots]
            match, gate = slot_gate(part[:, 2 * feat :], names[e], top)
            grad = part[:, feat : 2 * feat]
            xs[e, here, :] = part[:, :feat].astype(BF16)
            us[e, here, :] = grad.astype(BF16)
            gs[e, here, :] = (gate * grad).astype(BF16)
            metas[e, here, :] = jnp.where(match, gate, 0.0)
    s_lane = lax.broadcasted_iota(jnp.int32, (slots, LANES), 1)
    own = pl.ds(pl.multiple_of(block_at * slots, slots), slots)
    columns = feat // GROUPS
    cols = pl.ds(pl.multiple_of(block_at * columns, columns), columns)
    each = columns // CLASS
    back = []
    for a in range(CORES):
        copies[2 * a].wait()
        copies[2 * a + 1].wait()
        for j in range(local):
            e = a * local + j
            act, hg = through_expert(xs[e], gs[e], up_ref[e], down_ref[e])
            acts[...] = act
            hgs[...] = hg
            kept = metas[e, own, :]
            gate = jnp.max(kept, axis=1, keepdims=True)
            out = dot(acts[own, :], down_ref[e], NN).astype(BF16).astype(F32)
            dots = jnp.sum(us[e, own, :].astype(F32) * out, axis=1, keepdims=True)
            high = dots.astype(BF16).astype(F32)
            d = jnp.where(kept > 0.0, jnp.where(s_lane < top, high, dots - high), 0.0)
            rg = dot(hgs[own, :], up_ref[e], NN).astype(BF16)
            back.append(jnp.concatenate([(gate * out).astype(BF16), d.astype(BF16), rg], axis=1))
            for m, (side, value) in enumerate(((xs, hgs), (gs, acts))):
                sums[...] = dot(side[e, :, cols], value[...], TN).astype(BF16)
                for q in range(CLASS):
                    take = pl.ds(pl.multiple_of((spot ^ q) * each, each), each)
                    (keep_out, give_out)[a][q % 2, q // 2, m, j] = sums[take, :]
    stacked = jnp.concatenate(back, axis=0)
    result_ref[...] = dot(picked[block_at], stacked, NN).astype(BF16)
    share = rows // Y
    for y in range(Y):
        start = pl.multiple_of(((y_at + Y - y) % Y) * share, share)
        back_out[y * share : (y + 1) * share, :] = result_ref[pl.ds(start, share), :]


VMEM = pl.BlockSpec(memory_space=pltpu.VMEM)
HBM = pl.BlockSpec(memory_space=pltpu.HBM)
SCALARS = pl.BlockSpec(memory_space=pltpu.SMEM)


def run_experts(pieces, weights, where, tok, feat, top):
    local, units, _ = weights[0].shape
    width = pieces[0].shape[1]
    experts = CORES * local
    rows = pieces[0].shape[0] // GROUPS * Y
    slots = rows // tok * CAPACITY
    parts = jax.ShapeDtypeStruct((2, 2, 2, local, feat // Z_LO, units), BF16)
    return pl.pallas_call(
        functools.partial(experts_kernel, tok=tok, feat=feat, local=local, top=top),
        out_shape=(
            jax.ShapeDtypeStruct((rows, width), BF16),
            parts,
            parts,
        ),
        in_specs=[SCALARS] + [HBM] * (len(pieces) + len(weights)),
        out_specs=(VMEM,) * 3,
        scratch_shapes=[
            pltpu.VMEM((Y, pieces[0].shape[0], width), BF16),
            pltpu.VMEM((experts, units, feat), BF16),
            pltpu.VMEM((experts, units, feat), BF16),
            pltpu.VMEM((experts, GROUPS * slots, feat), BF16),
            pltpu.VMEM((experts, GROUPS * slots, feat), BF16),
            pltpu.VMEM((experts, GROUPS * slots, feat), BF16),
            pltpu.VMEM((GROUPS, rows, experts * slots), BF16),
            pltpu.VMEM((experts, GROUPS * slots, LANES), F32),
            pltpu.VMEM((GROUPS * slots, units), BF16),
            pltpu.VMEM((GROUPS * slots, units), BF16),
            pltpu.VMEM((rows, width), BF16),
            pltpu.VMEM((feat // GROUPS, units), BF16),
            pltpu.SemaphoreType.DMA((len(pieces) + 2,)),
            pltpu.SemaphoreType.DMA((2, CORES)),
        ],
        compiler_params=pltpu.CompilerParams(vmem_limit_bytes=44 * 1024 * 1024),
        cost_estimate=pl.CostEstimate(
            flops=12 * 10**9, bytes_accessed=20 * 10**6, transcendentals=10**6
        ),
    )(where, *pieces, *weights)


def both_halves(kept, got):
    return (kept.astype(F32) + got.astype(F32)).astype(BF16)


def body(sections, tokens, routes, gate_values, up_weight, down_weight, out_grad):
    tok, feat = tokens.shape[1:]
    top = routes.shape[2]
    gates = gate_values[0]
    names = routes[0].astype(BF16)
    high = lax.reduce_precision(gates, 8, 7)
    copies = CORES * up_weight.shape[1]
    gap = jnp.zeros((tok, GATES_AT - copies * top), BF16)
    meta = jnp.concatenate(
        [names] * copies + [gap, high.astype(BF16), (gates - high).astype(BF16)], axis=1
    )
    meta = jnp.pad(meta, ((0, 0), (0, LANES - meta.shape[1])))
    mine = jnp.concatenate([tokens[0], out_grad[0], meta], axis=1)

    z_lo = lax.axis_index("dp")
    position = lax.axis_index("expert")
    local = up_weight.shape[1]
    other = position + 1 - 2 * (position % CORES)
    first = [p * local + j for p in (position, other) for j in range(local)]
    y_at = position // (CORES * Z_HI)
    where = jnp.stack(first + [z_lo // CLASS, y_at, z_lo % CLASS]).astype(jnp.int32)
    up_t, down = jnp.swapaxes(up_weight[0], 1, 2), down_weight[0]

    line = gather(mine, Z_CLASSES)
    head = 2 * tok
    early = gather(line[:head], Y_RINGS)
    left, right = send(line[head:], dy=1), send(line[head:], dy=-1)
    middle = (line.shape[0] - head) // 32 * 16 + 16
    far_left, far_right = send(left[:middle], dy=1), send(right[middle:], dy=-1)
    weights = [up_t, down]
    up_t, down, *_ = lax.optimization_barrier((up_t, down, left, right))
    weights = weights + [send(up_t, flip=1), send(down, flip=1)]
    back, keep, give = run_experts(
        [line, early, left, right, far_left, far_right], weights, where, tok, feat, top
    )

    share = back.shape[0] // Y
    spread = lax.all_to_all(back, PLANE, 0, 0, tiled=True, axis_index_groups=Y_RINGS)
    total = jnp.sum(spread.reshape(Y, share, -1).astype(F32), axis=0).astype(BF16)
    below = (position // CORES) % Z_HI == 0
    inner = jnp.where(below, total[:tok], total[tok:])
    outer = jnp.where(below, total[tok:], total[:tok])

    got = send(give, flip=1)
    give = both_halves(keep[1], got[1])
    keep = both_halves(keep[0], got[0])
    got = send(give, block_flip=1)
    give = both_halves(keep[1], got[1])
    keep = both_halves(keep[0], got[0])
    last = send(give, block_flip=2)
    beyond = send(outer, dz=Z_LO)
    beyond, give = lax.optimization_barrier((beyond, give))
    added = inner.astype(F32) + beyond.astype(F32)
    dots = added[:, feat : feat + LANES]
    gate_grad = dots[:, :top] + dots[:, top : 2 * top]
    input_grad = send_to_section_before(added[:, feat + LANES :].astype(BF16), sections)
    sums = both_halves(keep, last)
    return (
        added[:, :feat].astype(BF16)[None],
        input_grad[None],
        gate_grad[None],
        sums[0][None],
        sums[1][None],
    )


def solution(mesh):
    placed = (
        P("section", ("dp", "expert"), None),
        P("section", ("dp", "expert"), None),
        P("section", ("dp", "expert"), None),
        P("section", "expert", None, None),
        P("section", "expert", None, None),
        P("section", ("dp", "expert"), None),
    )
    return jax.shard_map(
        functools.partial(body, mesh.shape["section"]),
        mesh=mesh,
        in_specs=placed,
        out_specs=(
            P("section", ("dp", "expert"), None),
            P("section", ("dp", "expert"), None),
            P("section", ("dp", "expert"), None),
            P("section", "expert", "dp", None),
            P("section", "expert", "dp", None),
        ),
        check_vma=False,
    )
```
